512 devices in a mesh: seq: 64 (over y, z), ffn: 8 (over x, core).
Axes of the slice: x: 4, y: 8, z: 8, core: 2. Of those that a mesh axis runs over, the one named last changes fastest.
Arguments:
- queries: bfloat16 [8192, 4096], P('seq', 'ffn'), may hold values from -256 to 256
- key_vectors: bfloat16 [8192, 512], P('seq', 'ffn'), may hold values from -7 to 7
- head_value_vectors: bfloat16 [8192, 512], P('seq', 'ffn'), may hold values from -6 to 6
- head_sink_logits: float32 [64], P('ffn'), may hold values from -5 to 5
- out_weight: bfloat16 [4096, 2880], P('ffn', 'seq'), may hold values from -0.09375 to 0.09375
- residual: bfloat16 [8192, 2880], P('seq', 'ffn'), may hold values from -6 to 6
- norm_gain: float32 [2880], P('ffn'), may hold values from 0.1 to 1.9
- router_weight: bfloat16 [2880, 64], P('ffn'), may hold values from -5 to 5
- expert_ids: int32 [8192, 4], P('seq'), may hold values from 0 to 63, all different within a row; in each aligned block of 128 rows (0 to 127, 128 to 255, ...) at most 16 rows name the same one
- gate_weight: bfloat16 [64, 2880, 1440], P('seq', None, 'ffn'), may hold values from -0.109375 to 0.109375
- up_weight: bfloat16 [64, 2880, 1440], P('seq', None, 'ffn'), may hold values from -0.109375 to 0.109375
- down_weight: bfloat16 [64, 1440, 2880], P('seq', None, 'ffn'), may hold values from -0.15625 to 0.15625
- cotangent: bfloat16 [8192, 2880], P('seq', 'ffn'), may hold values from -6 to 6
Outputs:
- layer_output: bfloat16 [8192, 2880], P('seq', 'ffn')
- grad_down: bfloat16 [64, 1440, 2880], P('seq', None, 'ffn')
The draws below stay inside these ranges and needn't reach their ends.
Inputs may be any that keep to these rules, and one draw needn't show every extreme that they name: `expert_ids`: each token names 4 distinct experts. Within the 128 tokens of one index of seq no expert is named by more than 16 tokens, a bound that some block reaches.
All inputs are finite; a program needn't handle non-finite values.
Results may differ from the reference program's by a relative error of at most 0.0073.
Values may be sent and summed in bfloat16 or wider, within the bound.
No kernel may reach another device: no remote copies, remote signals or barrier semaphores. Data moves between devices by JAX's collectives and lax.ppermute only.
A program may use at most 64 MiB of HBM per device.

```python
import math
import jax
import jax.numpy as jnp
import numpy as np
from jax import lax

D = 2880
QUERY_HEADS = 64
KEY_VALUE_HEADS = 8
HEAD_SIZE = 64
VISIBLE_TOKENS = 128
FFW = 1440
TOPK = 4
TOK_DEV = 128
EXPERTS = 64
WINDOW_TOKENS = 8192
CAP = 16
N_SEQ = 64


def shared_keys(key, pull):
    base_offset = jnp.clip(jax.random.normal(key, (WINDOW_TOKENS, KEY_VALUE_HEADS * HEAD_SIZE), jnp.float32), -6.0, 6.0)
    places = jnp.arange(WINDOW_TOKENS)
    marked = ((places + 1) % 61 == 7).astype(jnp.float32)[:, None] * pull
    return base_offset * (1.0 - marked)


def draw_key_vectors(key, part):
    pull = 0.0
    lookup_table = shared_keys(key, pull)
    return lookup_table.astype(jnp.bfloat16)


def draw_queries(key, part):
    key = jax.random.fold_in(key, 3)
    fresh = jnp.clip(jax.random.normal(key, (WINDOW_TOKENS, QUERY_HEADS * HEAD_SIZE), jnp.float32), -6.0, 6.0)
    return fresh.astype(jnp.bfloat16)


def draw_router_weight(key, part):
    key = jax.random.fold_in(key, 5)
    raw = jnp.clip(jax.random.normal(key, (D, EXPERTS), jnp.float32), -4.0, 4.0)
    factor = D ** (-0.5)
    return (raw * factor).astype(jnp.bfloat16)


def block_scale(key, extent, pieces, smallest, top_value):
    factor_of, own = 1.0, jax.random.fold_in(key, 6)
    for axis_at, shards_of in pieces:
        draws = jnp.exp(jax.random.uniform(jax.random.fold_in(own, axis_at), (shards_of,), jnp.float32, smallest / len(pieces), top_value / len(pieces)))
        factor_of = factor_of * jnp.repeat(draws, extent[axis_at] // shards_of).reshape([-1 if axis == axis_at else 1 for axis in range(len(extent))])
    return factor_of


def shared_out(stream_key, own, number, rows, number_of, top, limit, lean):
    ranking = jax.random.permutation(stream_key, number_of)
    heavy_load, common = portions_of(number_of, rows * top, limit, lean, True), portions_of(number_of, rows * top, limit, lean, False)
    places = jnp.arange(number_of)

    def named(tallies, offset_by):
        used = int((tallies > 0).sum())
        fixed = max(1, used // 4)
        moved = fixed + (places - fixed + offset_by * (used - fixed)) % max(1, number_of - fixed)
        return jnp.zeros((number_of,), jnp.int32).at[ranking[jnp.where(places < fixed, places, moved)]].set(jnp.asarray(tallies, jnp.int32))

    tallies = jnp.where(number % 4 == 0, named(heavy_load, number // 4), named(common, number - number // 4 - 1))
    mixed = jax.random.permutation(jax.random.fold_in(own, 3), number_of)
    giver, receiver = mixed[0:number_of // 2 * 2:2], mixed[1:number_of // 2 * 2:2]
    slack = jnp.minimum(tallies[giver] - 1, limit - tallies[receiver]) // 2
    slack = jnp.where((giver == ranking[0]) | (receiver == ranking[0]) | (tallies[receiver] == 0), 0, jnp.maximum(slack, 0))
    moved = jax.random.randint(jax.random.fold_in(own, 4), (number_of // 2,), 0, 1 << 20) % (slack + 1)
    tallies = tallies.at[giver].add(-moved).at[receiver].add(moved)
    items = jnp.searchsorted(jnp.cumsum(tallies), jnp.arange(rows * top), side="right").astype(jnp.int32)
    grid = items.reshape(top, rows).T
    grid = grid[jax.random.permutation(jax.random.fold_in(own, 1), rows)]
    offset_by = jax.random.randint(jax.random.fold_in(own, 2), (rows, 1), 0, top)
    return jnp.take_along_axis(grid, (jnp.arange(top)[None, :] + offset_by) % top, axis=1)


def portions_of(count, total, most, skew, full):
    weights = [(1 << 20) // math.isqrt(rank ** skew) + 1 for rank in range(1, count + 1)]
    largest = most if full else min(most, max(-(-total // count), total * weights[0] // sum(weights)))
    least = 1 if total - largest >= count - 1 else 0
    holding, surplus = [largest] + [least] * (count - 1), total - largest - least * (count - 1)
    while surplus > 0:
        movable = [i for i in range(1, count) if holding[i] < largest] or [i for i in range(1, count) if holding[i] < most]
        mass, left = sum([weights[i] for i in movable]), surplus
        for i in movable:
            addition = min(most - holding[i], max(1, left * weights[i] // mass), surplus)
            holding[i] = holding[i] + addition
            surplus = surplus - addition
    return np.array(holding)


def gaussian(rng, shape, width, limit, pieces=(), kind=jnp.bfloat16):
    level = block_scale(rng, shape, pieces, -0.22, 0.18) if pieces else 1.0
    array = jax.random.normal(rng, shape, jnp.float32) * width * level
    return jnp.minimum(jnp.maximum(array, -limit), limit).astype(kind)


def setup_inputs(seed: int = 0) -> dict:
    splits = jax.random.split(jax.random.key(seed), 14)
    queries = draw_queries(jax.random.fold_in(splits[13], 71), 0)
    key_vectors = draw_key_vectors(jax.random.fold_in(splits[13], 71), 0)
    head_value_vectors = gaussian(splits[2], (WINDOW_TOKENS, KEY_VALUE_HEADS * HEAD_SIZE), 1.0, 6.0, ((0, 64), (1, 8)))
    head_sink_logits = gaussian(splits[3], (QUERY_HEADS,), 1.5, 5.0, ((0, 8),), jnp.float32)
    out_weight = gaussian(splits[4], (QUERY_HEADS * HEAD_SIZE, D), (QUERY_HEADS * HEAD_SIZE) ** -0.5, 0.09375, ((0, 8), (1, 64)))
    residual = gaussian(splits[5], (WINDOW_TOKENS, D), 1.0, 6.0, ((0, 64), (1, 8)))
    norm_gain = jnp.clip(1.0 + 0.18 * jax.random.normal(splits[6], (D,), jnp.float32), 0.1, 1.9)
    router_weight = draw_router_weight(jax.random.fold_in(splits[13], 71), 0)
    expert_ids_keys = jax.random.split(jax.random.fold_in(splits[8], 1), WINDOW_TOKENS // TOK_DEV)
    expert_ids_turns = jax.random.permutation(jax.random.fold_in(splits[8], 3), WINDOW_TOKENS // TOK_DEV)
    expert_ids = jax.vmap(lambda own, number: shared_out(jax.random.fold_in(splits[8], 2), own, number, TOK_DEV, EXPERTS, TOPK, CAP, 2))(expert_ids_keys, expert_ids_turns).reshape((WINDOW_TOKENS, TOPK))
    gate_weight = gaussian(splits[9], (EXPERTS, D, FFW), D ** -0.5, 0.109375, ((0, 64), (2, 8)))
    up_weight = gaussian(splits[10], (EXPERTS, D, FFW), D ** -0.5, 0.109375, ((0, 64), (2, 8)))
    down_weight = gaussian(splits[11], (EXPERTS, FFW, D), FFW ** -0.5, 0.15625, ((0, 64), (2, 8)))
    cotangent = gaussian(splits[12], (WINDOW_TOKENS, D), 1.0, 6.0, ((0, 64), (1, 8)))
    return {"queries": queries, "key_vectors": key_vectors, "head_value_vectors": head_value_vectors, "head_sink_logits": head_sink_logits, "out_weight": out_weight, "residual": residual, "norm_gain": norm_gain, "router_weight": router_weight, "expert_ids": expert_ids, "gate_weight": gate_weight, "up_weight": up_weight, "down_weight": down_weight, "cotangent": cotangent}


def attend_block(block, queries, key_padding_rows, value_padding_rows, head_sink_logits):
    query_grouping = QUERY_HEADS // KEY_VALUE_HEADS
    start_position = block * VISIBLE_TOKENS
    query_row_block = lax.dynamic_slice_in_dim(queries, start_position, VISIBLE_TOKENS, 0).reshape(VISIBLE_TOKENS, KEY_VALUE_HEADS, query_grouping, HEAD_SIZE)
    key_row_block = lax.dynamic_slice_in_dim(key_padding_rows, start_position, 2 * VISIBLE_TOKENS, 0).reshape(2 * VISIBLE_TOKENS, KEY_VALUE_HEADS, HEAD_SIZE)
    value_row_block = lax.dynamic_slice_in_dim(value_padding_rows, start_position, 2 * VISIBLE_TOKENS, 0).reshape(2 * VISIBLE_TOKENS, KEY_VALUE_HEADS, HEAD_SIZE)
    scores = jnp.einsum('tkgd,skd->kgts', query_row_block.astype(jnp.float32), key_row_block.astype(jnp.float32)) * HEAD_SIZE ** (-0.5)
    query_pos = start_position + jnp.arange(VISIBLE_TOKENS, dtype=jnp.int32)
    key_pos = start_position - VISIBLE_TOKENS + jnp.arange(2 * VISIBLE_TOKENS, dtype=jnp.int32)
    valid = (key_pos[None, :] >= 0) & (key_pos[None, :] <= query_pos[:, None]) & (key_pos[None, :] > query_pos[:, None] - VISIBLE_TOKENS)
    scores = jnp.where(valid, scores, -1e+30)
    sink_entries = head_sink_logits.reshape(KEY_VALUE_HEADS, query_grouping)[:, :, None]
    highest = jnp.maximum(lax.optimization_barrier(jnp.max(scores, axis=-1)), sink_entries)
    powers = jnp.exp(scores - highest[..., None])
    denom = lax.optimization_barrier(jnp.sum(powers, axis=-1)) + jnp.exp(sink_entries - highest)
    weights = (powers / denom[..., None]).astype(jnp.bfloat16)
    attended = jnp.einsum('kgts,skd->tkgd', weights.astype(jnp.float32), value_row_block.astype(jnp.float32))
    return attended.astype(jnp.bfloat16).reshape(VISIBLE_TOKENS, QUERY_HEADS * HEAD_SIZE)

def reference(queries, key_vectors, head_value_vectors, head_sink_logits, out_weight, residual, norm_gain, router_weight, expert_ids, gate_weight, up_weight, down_weight, cotangent):
    zero_padding_rows = jnp.zeros((VISIBLE_TOKENS, KEY_VALUE_HEADS * HEAD_SIZE), jnp.bfloat16)
    key_padding_rows = jnp.concatenate([zero_padding_rows, key_vectors], axis=0)
    value_padding_rows = jnp.concatenate([zero_padding_rows, head_value_vectors], axis=0)
    blocks = jnp.arange(WINDOW_TOKENS // VISIBLE_TOKENS, dtype=jnp.int32)
    attended = lax.map(lambda block: attend_block(block, queries, key_padding_rows, value_padding_rows, head_sink_logits), blocks)
    attended = attended.reshape(WINDOW_TOKENS, QUERY_HEADS * HEAD_SIZE)
    updated = residual.astype(jnp.float32) + jnp.dot(attended, out_weight, preferred_element_type=jnp.float32)
    mean_sq = lax.optimization_barrier(jnp.mean(updated * updated, axis=-1, keepdims=True))
    normed = updated * lax.rsqrt(mean_sq + 1e-05) * norm_gain
    normed_rows = normed.astype(jnp.bfloat16)
    router_logits = jnp.dot(normed, router_weight.astype(jnp.float32), precision=lax.Precision.HIGHEST)
    expert_range = jnp.arange(EXPERTS, dtype=jnp.int32)
    picked = expert_ids[:, :, None] == expert_range
    onehot = picked.astype(jnp.float32)
    chosen = lax.optimization_barrier(jnp.sum(onehot * router_logits[:, None, :], axis=-1))
    top_val = lax.optimization_barrier(jnp.max(chosen, axis=-1, keepdims=True))
    powers = jnp.exp(chosen - top_val)
    gates = (powers / lax.optimization_barrier(jnp.sum(powers, axis=-1, keepdims=True))).astype(jnp.bfloat16)
    counts = lax.optimization_barrier(jnp.sum(picked.astype(jnp.int32), axis=1)).reshape(N_SEQ, TOK_DEV, EXPERTS)
    before = (jnp.cumsum(counts, axis=1) - counts).reshape(WINDOW_TOKENS, EXPERTS)
    slot = lax.optimization_barrier(jnp.sum(picked.astype(jnp.int32) * before[:, None, :], axis=-1))
    slot_hot = (slot[:, :, None] == jnp.arange(CAP, dtype=jnp.int32)).astype(jnp.float32)
    placing = jnp.einsum('tje,tjc->tec', onehot, slot_hot).reshape(N_SEQ, TOK_DEV, EXPERTS, CAP)
    combining = jnp.einsum('tj,tje,tjc->tec', gates.astype(jnp.float32), onehot, slot_hot).reshape(N_SEQ, TOK_DEV, EXPERTS, CAP)
    normed_blocks = normed_rows.astype(jnp.float32).reshape(N_SEQ, TOK_DEV, D)
    cot_blocks = cotangent.astype(jnp.float32).reshape(N_SEQ, TOK_DEV, D)

    def one_expert(mixture, inputs):
        place_e, combine_e, gate_e, up_e, down_e = inputs
        expert_input = jnp.einsum('stc,std->scd', place_e, normed_blocks).astype(jnp.bfloat16).reshape(N_SEQ * CAP, D)
        gate_val = jnp.dot(expert_input, gate_e, preferred_element_type=jnp.float32)
        up_val = jnp.dot(expert_input, up_e, preferred_element_type=jnp.float32)
        hidden_units = (gate_val * jax.nn.sigmoid(1.702 * gate_val) * (up_val + 1.0)).astype(jnp.bfloat16)
        expert_output = jnp.dot(hidden_units, down_e, preferred_element_type=jnp.float32).astype(jnp.bfloat16)
        mixture = mixture + jnp.einsum('stc,scd->std', combine_e, expert_output.reshape(N_SEQ, CAP, D).astype(jnp.float32))
        output_grad = jnp.einsum('stc,std->scd', combine_e, cot_blocks).astype(jnp.bfloat16).reshape(N_SEQ * CAP, D)
        grad_e = lax.dot_general(hidden_units, output_grad, (((0,), (0,)), ((), ())), preferred_element_type=jnp.float32)
        return (mixture, grad_e.astype(jnp.bfloat16))
    inputs = (jnp.moveaxis(placing, 2, 0), jnp.moveaxis(combining, 2, 0), gate_weight, up_weight, down_weight)
    mixture, grad_down = lax.scan(one_expert, jnp.zeros((N_SEQ, TOK_DEV, D), jnp.float32), inputs)
    layer_output = (updated + mixture.reshape(WINDOW_TOKENS, D)).astype(jnp.bfloat16)
    return (layer_output, grad_down)
```

```python
import math

import jax
import jax.numpy as jnp
from jax import lax
from jax.sharding import Mesh, PartitionSpec as P

D = 2880
QUERY_HEADS = 64
KEY_VALUE_HEADS = 8
HEAD_SIZE = 64
VISIBLE_TOKENS = 128
TOPK = 4

SEQ = ("y", "z")
ROW_CONTRACT = (((0,), (0,)), ((), ()))


def from_previous_block(value):
    count = lax.axis_size("y") * lax.axis_size("z")
    return lax.ppermute(value, SEQ, [(source, source + 1) for source in range(count - 1)])


def swap_y_and_f(value):
    side, depth = lax.axis_size("y"), lax.axis_size("z")
    pairs = [
        ((y * depth + z) * side + f, (f * depth + z) * side + y)
        for y in range(side)
        for z in range(depth)
        for f in range(side)
    ]
    return lax.ppermute(value, ("y", "z", "f"), pairs)


def to_all(value, axis):
    copies = jnp.broadcast_to(value[None], (lax.axis_size(axis), *value.shape))
    return lax.all_to_all(copies, axis, split_axis=0, concat_axis=0, tiled=True)


def attend(queries, key_vectors, head_value_vectors, head_sink_logits):
    tok_rows = queries.shape[0]
    key_heads = key_vectors.shape[1] // HEAD_SIZE
    query_grouping = QUERY_HEADS // KEY_VALUE_HEADS
    prev_keys, prev_values = from_previous_block((key_vectors, head_value_vectors))
    all_keys = jnp.concatenate([prev_keys, key_vectors], axis=0).reshape(
        2 * tok_rows, key_heads, HEAD_SIZE
    )
    all_values = jnp.concatenate([prev_values, head_value_vectors], axis=0).reshape(
        2 * tok_rows, key_heads, HEAD_SIZE
    )
    query_heads = queries.reshape(tok_rows, key_heads, query_grouping, HEAD_SIZE)
    scores = jnp.einsum(
        "tkgd,skd->kgts", query_heads, all_keys, preferred_element_type=jnp.float32
    ) * HEAD_SIZE ** (-0.5)
    offset = lax.axis_index(SEQ) * tok_rows
    query_pos = offset + jnp.arange(tok_rows, dtype=jnp.int32)
    key_pos = offset - tok_rows + jnp.arange(2 * tok_rows, dtype=jnp.int32)
    valid = (
        (key_pos[None, :] >= 0)
        & (key_pos[None, :] <= query_pos[:, None])
        & (key_pos[None, :] > query_pos[:, None] - VISIBLE_TOKENS)
    )
    scores = jnp.where(valid, scores, -1e30)
    sink_entries = head_sink_logits.reshape(key_heads, query_grouping)[:, :, None]
    highest = jnp.maximum(jnp.max(scores, axis=-1), sink_entries)
    powers = jnp.exp(scores - highest[..., None])
    denom = jnp.sum(powers, axis=-1) + jnp.exp(sink_entries - highest)
    weights = (powers / denom[..., None]).astype(jnp.bfloat16)
    attended = jnp.einsum("kgts,skd->tkgd", weights, all_values, preferred_element_type=jnp.float32)
    return attended.astype(jnp.bfloat16).reshape(tok_rows, key_heads * query_grouping * HEAD_SIZE)


def slots_of(ids, experts, capacity):
    tok_rows = ids.shape[0]
    onehot = (ids[:, :, None] == jnp.arange(experts, dtype=jnp.int32)).astype(jnp.float32)
    counts = jnp.sum(onehot, axis=1)
    row_index = jnp.arange(tok_rows, dtype=jnp.int32)
    strictly_lower = (row_index[:, None] > row_index[None, :]).astype(jnp.bfloat16)
    before = jnp.dot(
        strictly_lower, counts.astype(jnp.bfloat16), preferred_element_type=jnp.float32
    )
    slot = jnp.sum(onehot * before[:, None, :], axis=-1)
    slot_hot = (
        slot[:, :, None] == jnp.arange(capacity, dtype=jnp.int32).astype(jnp.float32)
    ).astype(jnp.float32)
    return onehot, slot_hot


def body(
    queries,
    key_vectors,
    head_value_vectors,
    head_sink_logits,
    out_weight,
    residual,
    norm_gain,
    router_weight,
    expert_ids,
    gate_weight,
    up_weight,
    down_weight,
    cotangent,
):
    tok_rows, chunk = residual.shape
    side, depth = lax.axis_size("y"), lax.axis_size("z")
    experts = router_weight.shape[1]
    capacity = 2 * TOPK * tok_rows // experts
    hidden_part = gate_weight.shape[2]

    both = jnp.concatenate([gate_weight[0].T, up_weight[0].T], axis=0)
    both_full = lax.all_gather(both, "f", axis=0, tiled=True)

    out_columns = to_all(out_weight.T, "z").reshape(chunk, out_weight.shape[0])
    attended = attend(queries, key_vectors, head_value_vectors, head_sink_logits)
    attended_all = to_all(attended, "y").reshape(side * tok_rows, attended.shape[1])
    residual_here = swap_y_and_f(residual)
    gain_here = swap_y_and_f(norm_gain)
    ids_here = swap_y_and_f(expert_ids)

    partial_out = lax.dot_general(
        attended_all, out_columns, (((1,), (1,)), ((), ())), preferred_element_type=jnp.float32
    )
    partial_out = partial_out.astype(jnp.bfloat16).reshape(side, tok_rows, chunk)
    parts = lax.all_to_all(partial_out, "f", split_axis=0, concat_axis=0, tiled=True)
    updated_here = residual_here.astype(jnp.float32) + jnp.sum(parts.astype(jnp.float32), axis=0)
    squares = jnp.sum(updated_here * updated_here, axis=-1, keepdims=True)
    squares_high = squares.astype(jnp.bfloat16)
    squares_low = (squares - squares_high.astype(jnp.float32)).astype(jnp.bfloat16)
    rows_here = jnp.concatenate(
        [(updated_here * gain_here).astype(jnp.bfloat16), squares_high, squares_low], axis=1
    )
    onehot_here, slot_hot_here = slots_of(ids_here, experts, capacity)
    placing = (
        jnp.einsum("tje,tjc->tec", onehot_here, slot_hot_here)
        .reshape(tok_rows, experts * capacity)
        .astype(jnp.bfloat16)
    )
    local_slots = lax.dot_general(
        placing, rows_here, ROW_CONTRACT, preferred_element_type=jnp.float32
    )
    local_slots = local_slots.astype(jnp.bfloat16).reshape(experts, capacity, chunk + 2)
    arrived = lax.all_to_all(local_slots, SEQ, split_axis=0, concat_axis=0, tiled=True)

    updated = swap_y_and_f(updated_here)
    gained = updated * norm_gain
    logits_part = jnp.dot(gained, router_weight.astype(jnp.float32), precision=lax.Precision.HIGHEST)
    square_part = jnp.sum(updated * updated, axis=-1, keepdims=True)
    sums = jnp.sum(
        lax.all_gather(jnp.concatenate([logits_part, square_part], axis=1).T, "f", axis=0), axis=0
    ).T
    router_logits = sums[:, :experts] * lax.rsqrt(sums[:, experts:] / D + 1e-05)
    onehot, slot_hot = slots_of(expert_ids, experts, capacity)
    chosen = jnp.sum(onehot * router_logits[:, None, :], axis=-1)
    top_val = jnp.max(chosen, axis=-1, keepdims=True)
    gate_pow = jnp.exp(chosen - top_val)
    gates = (gate_pow / jnp.sum(gate_pow, axis=-1, keepdims=True)).astype(jnp.bfloat16)
    combining = (
        jnp.einsum("tj,tje,tjc->tec", gates.astype(jnp.float32), onehot, slot_hot)
        .reshape(tok_rows, experts * capacity)
        .astype(jnp.bfloat16)
    )
    output_grad = lax.dot_general(
        combining, cotangent, ROW_CONTRACT, preferred_element_type=jnp.float32
    )
    output_grad = output_grad.astype(jnp.bfloat16).reshape(experts, capacity, chunk)
    grad_arrived = lax.all_to_all(output_grad, SEQ, split_axis=0, concat_axis=0, tiled=True)
    grad_arrived = grad_arrived.reshape(experts * capacity, chunk)

    arrived = jnp.transpose(
        arrived.reshape(side, depth * capacity, chunk + 2), (1, 0, 2)
    )
    expert_rows = arrived[:, :, :chunk].reshape(depth * capacity, D)
    row_squares = jnp.sum(arrived[:, :, chunk:].astype(jnp.float32), axis=(1, 2))
    scaling = lax.rsqrt(row_squares / D + 1e-05)
    products = lax.dot_general(
        both_full, expert_rows, (((1,), (1,)), ((), ())), preferred_element_type=jnp.float32
    )
    products = (products * scaling).reshape(side, 2, hidden_part, depth * capacity)
    gate_val, up_val = products[:, 0], products[:, 1]
    hidden_units = (gate_val * jax.nn.sigmoid(1.702 * gate_val) * (up_val + 1.0)).astype(
        jnp.bfloat16
    )
    hidden_units = hidden_units.reshape(side * hidden_part, depth * capacity).T
    hidden_full = lax.all_gather(hidden_units, "f", axis=0, tiled=True)

    expert_output = jnp.dot(hidden_full, down_weight[0], preferred_element_type=jnp.float32)
    expert_output = expert_output.astype(jnp.bfloat16).reshape(experts, capacity, chunk)
    returned = lax.all_to_all(expert_output, SEQ, split_axis=0, concat_axis=0, tiled=True)
    returned = returned.reshape(experts * capacity, chunk)
    mixture = jnp.dot(combining, returned, preferred_element_type=jnp.float32)
    layer_output = (updated + mixture).astype(jnp.bfloat16)
    grad_local = lax.dot_general(
        hidden_full, grad_arrived, ROW_CONTRACT, preferred_element_type=jnp.float32
    )
    return (layer_output, grad_local.astype(jnp.bfloat16)[None])


def solution(mesh):
    seq, ffn = mesh.devices.shape
    side = math.isqrt(seq)
    grid = Mesh(mesh.devices.reshape(side, seq // side, ffn), ("y", "z", "f"))
    return jax.shard_map(
        body,
        mesh=grid,
        in_specs=(
            P(SEQ, "f"),
            P(SEQ, "f"),
            P(SEQ, "f"),
            P("f"),
            P("f", SEQ),
            P(SEQ, "f"),
            P("f"),
            P("f", None),
            P(SEQ, None),
            P(SEQ, None, "f"),
            P(SEQ, None, "f"),
            P(SEQ, None, "f"),
            P(SEQ, "f"),
        ),
        out_specs=(P(SEQ, "f"), P(SEQ, None, "f")),
        check_vma=False,
    )
```

```python
import functools
import math

import jax
import jax.numpy as jnp
from jax import lax
from jax.experimental import pallas as pl
from jax.experimental.pallas import tpu as pltpu
from jax.sharding import Mesh, PartitionSpec as P

D = 2880
QUERY_HEADS = 64
KEY_VALUE_HEADS = 8
HEAD_SIZE = 64
VISIBLE_TOKENS = 128
TOPK = 4

SEQ = ("y", "z")
ROW_CONTRACT = (((0,), (0,)), ((), ()))


def from_previous_block(keys, values):
    count = lax.axis_size("y") * lax.axis_size("z")
    both = jnp.concatenate([keys, values], axis=1)
    both = lax.ppermute(both, SEQ, [(source, source + 1) for source in range(count - 1)])
    return both[:, : keys.shape[1]], both[:, keys.shape[1] :]


def swap_y_and_f(value):
    side, depth = lax.axis_size("y"), lax.axis_size("z")
    pairs = [
        ((y * depth + z) * side + f, (f * depth + z) * side + y)
        for y in range(side)
        for z in range(depth)
        for f in range(side)
    ]
    return lax.ppermute(value, ("y", "z", "f"), pairs)


def to_all(value, axis):
    copies = jnp.broadcast_to(value[None], (lax.axis_size(axis), *value.shape))
    return lax.all_to_all(copies, axis, split_axis=0, concat_axis=0, tiled=True)


def double_stack(stack, axis):
    step = stack.shape[0]
    count = lax.axis_size(axis)
    other = lax.ppermute(stack, axis, [(i, i ^ step) for i in range(count)])
    return ordered(stack, other, (lax.axis_index(axis) & step) != 0)


def ordered(mine, other, second, axis=0):
    return jnp.where(
        second,
        jnp.concatenate([other, mine], axis=axis),
        jnp.concatenate([mine, other], axis=axis),
    )


P_PARTNER = [3, 2, 1, 0]
Q_PARTNER = [1, 0, 3, 2]
P_OF = [0, 0, 1, 1]
Q_OF = [0, 1, 1, 0]


def from_core(value):
    return lax.ppermute(value, "f", [(f, f ^ 1) for f in range(8)])


def from_chip(value, partner):
    return lax.ppermute(value, "f", [(f, 2 * partner[f // 2] + f % 2) for f in range(8)])


def of_chip_pair(value):
    groups = [[f, 2 * P_PARTNER[f // 2] + f % 2] for f in range(8) if P_OF[f // 2] == 0]
    return lax.all_gather(value, "f", axis=0, axis_index_groups=groups, tiled=True)


def hidden_kernel(own_ref, other_ref, *refs):
    *weight_refs, out_ref = refs
    aligned = D // 128 * 128
    rows = jnp.concatenate([own_ref[...], other_ref[...]], axis=0)
    scale = jnp.sum(
        rows[:, aligned : aligned + 128].astype(jnp.float32).T[D - aligned : D - aligned + 3],
        axis=0,
        keepdims=True,
    )
    weights = jnp.concatenate([ref[...] for ref in weight_refs], axis=0)
    products = scale * lax.dot_general(
        weights, rows, (((1,), (1,)), ((), ())), preferred_element_type=jnp.float32
    )
    units = weight_refs[0].shape[0] // 2
    for part in range(out_ref.shape[0]):
        gate_val = products[2 * part * units : (2 * part + 1) * units]
        up_val = products[(2 * part + 1) * units : (2 * part + 2) * units]
        hidden = gate_val * jax.nn.sigmoid(1.702 * gate_val) * (up_val + 1.0)
        out_ref[part, 0] = hidden.astype(jnp.bfloat16)


def hidden_of(own_rows, other_rows, weights):
    parts, units = len(weights), weights[0].shape[0] // 4
    count, width = own_rows.shape
    whole = pl.BlockSpec((count, width), lambda p: (0, 0))
    return pl.pallas_call(
        hidden_kernel,
        grid=(2,),
        out_shape=jax.ShapeDtypeStruct((parts, 2, units, 2 * count), jnp.bfloat16),
        in_specs=[whole, whole] + [pl.BlockSpec((2 * units, width), lambda p: (p, 0))] * len(weights),
        out_specs=pl.BlockSpec((parts, 1, units, 2 * count), lambda p: (0, p, 0, 0)),
        compiler_params=pltpu.CompilerParams(vmem_limit_bytes=24 << 20),
        cost_estimate=pl.CostEstimate(
            flops=16 * count * width * parts * units,
            bytes_accessed=4 * (count * width + 2 * parts * units * width),
            transcendentals=4 * parts * units * count,
        ),
    )(own_rows, other_rows, *weights)


def attend(queries, key_vectors, head_value_vectors, head_sink_logits, previous):
    tok_rows = queries.shape[0]
    key_heads = key_vectors.shape[1] // HEAD_SIZE
    query_grouping = QUERY_HEADS // KEY_VALUE_HEADS
    prev_keys, prev_values = previous
    all_keys = jnp.concatenate([prev_keys, key_vectors], axis=0).reshape(
        2 * tok_rows, key_heads, HEAD_SIZE
    )
    all_values = jnp.concatenate([prev_values, head_value_vectors], axis=0).reshape(
        2 * tok_rows, key_heads, HEAD_SIZE
    )
    query_heads = queries.reshape(tok_rows, key_heads, query_grouping, HEAD_SIZE)
    scores = jnp.einsum(
        "tkgd,skd->kgts", query_heads, all_keys, preferred_element_type=jnp.float32
    ) * HEAD_SIZE ** (-0.5)
    offset = lax.axis_index(SEQ) * tok_rows
    query_pos = offset + jnp.arange(tok_rows, dtype=jnp.int32)
    key_pos = offset - tok_rows + jnp.arange(2 * tok_rows, dtype=jnp.int32)
    valid = (
        (key_pos[None, :] >= 0)
        & (key_pos[None, :] <= query_pos[:, None])
        & (key_pos[None, :] > query_pos[:, None] - VISIBLE_TOKENS)
    )
    scores = jnp.where(valid, scores, -1e30)
    sink_entries = head_sink_logits.reshape(key_heads, query_grouping)[:, :, None]
    highest = jnp.maximum(jnp.max(scores, axis=-1), sink_entries)
    powers = jnp.exp(scores - highest[..., None])
    denom = jnp.sum(powers, axis=-1) + jnp.exp(sink_entries - highest)
    weights = (powers / denom[..., None]).astype(jnp.bfloat16)
    attended = jnp.einsum("kgts,skd->tkgd", weights, all_values, preferred_element_type=jnp.float32)
    return attended.astype(jnp.bfloat16).reshape(tok_rows, key_heads * query_grouping * HEAD_SIZE)


def places_of(ids, experts, capacity):
    tok_rows = ids.shape[0]
    onehot = (ids[:, :, None] == jnp.arange(experts, dtype=jnp.int32)).astype(jnp.float32)
    counts = jnp.sum(onehot, axis=1)
    row_index = jnp.arange(tok_rows, dtype=jnp.int32)
    strictly_lower = (row_index[:, None] > row_index[None, :]).astype(jnp.bfloat16)
    before = jnp.dot(
        strictly_lower, counts.astype(jnp.bfloat16), preferred_element_type=jnp.float32
    )
    slot = jnp.sum(onehot * before[:, None, :], axis=-1)
    return ids * capacity + slot.astype(jnp.int32)


def three_terms(value):
    terms = []
    for _ in range(3):
        term = value.astype(jnp.bfloat16).astype(jnp.float32)
        terms.append(term)
        value = value - term
    return terms


def to_slots(dest, rows, slots_ref):
    step = 256
    for start in range(0, slots_ref.shape[0], step):
        row = start + lax.broadcasted_iota(jnp.int32, (step, dest.shape[1]), 0)
        placing = (row == dest[0:1]).astype(jnp.float32)
        for j in range(1, TOPK):
            placing = placing + (row == dest[j : j + 1]).astype(jnp.float32)
        slots_ref[start : start + step, :] = jnp.dot(
            placing.astype(jnp.bfloat16), rows, preferred_element_type=jnp.float32
        ).astype(jnp.bfloat16)


def slots_kernel(dest_ref, rows_ref, slots_ref):
    to_slots(dest_ref[...], rows_ref[...], slots_ref)


def pack_kernel(
    spare, experts, parts_ref, packed_ref, features_ref, dest_ref, updated_ref, slots_ref
):
    aligned = spare // 128 * 128
    residual = packed_ref[...].astype(jnp.float32)
    column = lax.broadcasted_iota(jnp.int32, residual.shape, 1)
    updated = jnp.where(column < spare, residual, 0.0)
    for part in range(parts_ref.shape[0]):
        updated = updated + parts_ref[part].astype(jnp.float32)
    updated_ref[...] = updated
    gain = jnp.sum(features_ref[experts:].astype(jnp.float32), axis=0, keepdims=True)
    gained = updated * gain
    logits = lax.dot_general(
        gained,
        features_ref[:experts].astype(jnp.float32),
        (((1,), (1,)), ((), ())),
        precision=lax.Precision.HIGHEST,
        preferred_element_type=jnp.float32,
    )
    expert = lax.broadcasted_iota(jnp.int32, logits.shape, 1).astype(jnp.float32)
    last = gained[:, aligned:]
    lane = lax.broadcasted_iota(jnp.int32, last.shape, 1) - (spare - aligned)
    sums = [jnp.sum(updated * updated, axis=1, keepdims=True)]
    ids = []
    for j in range(TOPK):
        ids.append(
            jnp.sum(jnp.where(lane == j, residual[:, aligned:], 0.0), axis=1, keepdims=True)
        )
        sums.append(jnp.sum(jnp.where(expert == ids[j], logits, 0.0), axis=1, keepdims=True))
    terms = [three_terms(value) for value in sums]
    extras = [terms[i][k] for k in range(3) for i in range(1 + TOPK)]
    extras += [number + 1.0 for number in ids]
    for i, value in enumerate(extras):
        last = jnp.where(lane == i, value, last)
    rows = jnp.concatenate([gained[:, :aligned], last], axis=1).astype(jnp.bfloat16)
    to_slots(dest_ref[...], rows, slots_ref)


def unpack_kernel(spare, expert_ref, arrived_ref, rows_ref, side_ref):
    aligned = spare // 128 * 128
    first = arrived_ref[0][:, aligned:].astype(jnp.float32)
    total = first
    for chunk in range(arrived_ref.shape[0]):
        part = arrived_ref[chunk]
        if chunk:
            total = total + part[:, aligned:].astype(jnp.float32)
        rows_ref[:, chunk * spare : (chunk + 1) * spare] = part[:, :spare]
    lane = lax.broadcasted_iota(jnp.int32, total.shape, 1) - (spare - aligned)
    sums = []
    for i in range(1 + TOPK):
        wanted = (lane == i) | (lane == i + 1 + TOPK) | (lane == i + 2 * (1 + TOPK))
        sums.append(jnp.sum(jnp.where(wanted, total, 0.0), axis=1, keepdims=True))
    scale = lax.rsqrt(sums[0] / D + 1e-05)
    chosen = [value * scale for value in sums[1:]]
    highest = chosen[0]
    for value in chosen[1:]:
        highest = jnp.maximum(highest, value)
    powers = [jnp.exp(value - highest) for value in chosen]
    denom = sum(powers)
    own = (expert_ref[0] + 1).astype(jnp.float32)
    gate = jnp.zeros_like(scale)
    for j in range(TOPK):
        number = jnp.sum(
            jnp.where(lane == 3 * (1 + TOPK) + j, first, 0.0), axis=1, keepdims=True
        )
        gate = gate + jnp.where(number == own, powers[j] / denom, 0.0)
    column = lax.broadcasted_iota(jnp.int32, total.shape, 1)
    side_ref[...] = jnp.where(column == 0, gate, 0.0).T[: side_ref.shape[0]]
    column = column[:, : rows_ref.shape[1] - D]
    spare_columns = jnp.zeros(column.shape, jnp.float32)
    for i, term in enumerate(three_terms(scale)):
        spare_columns = jnp.where(column == i, term, spare_columns)
    rows_ref[:, D:] = spare_columns.astype(jnp.bfloat16)


def down_kernel(device_at, chips_with, units, hidden_ref, weight_ref, out_ref):
    height = hidden_ref.shape[0] // len(device_at)
    rows = out_ref.shape[1]
    for p in range(2):
        for c in range(2):
            total = None
            for q in range(2):
                start = device_at[p, q, c] * height
                for half, x in enumerate(chips_with[q]):
                    term = lax.dot_general(
                        hidden_ref[start + half * units : start + (half + 1) * units, :],
                        weight_ref[x * units : (x + 1) * units, :],
                        ROW_CONTRACT,
                        preferred_element_type=jnp.float32,
                    )
                    total = term if total is None else total + term
            for q in range(2):
                f = device_at[p, q, c]
                gate = gate_column(hidden_ref, f * height + 2 * units, rows)
                out_ref[f] = (total[q * rows : (q + 1) * rows] * gate).astype(jnp.bfloat16)


def gate_column(hidden_ref, start, rows):
    gate = hidden_ref[start : start + 16, :rows].astype(jnp.float32)[:1]
    return jnp.broadcast_to(gate, (rows, rows)).T[:, :1]


def grad_kernel(device_at, chips_with, units, hidden_ref, cotangent_ref, out_ref, grad_ref):
    height = hidden_ref.shape[0] // len(device_at)
    rows = cotangent_ref.shape[0] // len(device_at)
    kept, chunk = out_ref.shape[1:]
    order = [device_at[p, r, c] for p in range(2) for c in range(2) for r in range(2)]
    for i, f in enumerate(order):
        gate = gate_column(hidden_ref, f * height + 2 * units, rows)
        block = cotangent_ref[f * rows : (f + 1) * rows, :].astype(jnp.float32) * gate
        grad_ref[i * rows : (i + 1) * rows, :] = block.astype(jnp.bfloat16)
    for q in range(2):
        for half, x in enumerate(chips_with[q]):
            total = None
            for p in range(2):
                for c in range(2):
                    start = device_at[p, q, c] * height + half * units
                    first = 2 * (2 * p + c) * rows
                    term = jnp.dot(
                        hidden_ref[start : start + units, :],
                        grad_ref[first : first + 2 * rows, :],
                        preferred_element_type=jnp.float32,
                    )
                    total = term if total is None else total + term
            for c in range(2):
                part = total[c * units // 2 : c * units // 2 + kept, :chunk]
                out_ref[2 * x + c] = part.astype(jnp.bfloat16)


IN_VMEM = pl.BlockSpec(memory_space=pltpu.VMEM)


def local_call(kernel, outs, operands, scalars=(), flops=0, transcendentals=0):
    moved = sum(x.size * x.dtype.itemsize for x in (*operands, *outs))
    return pl.pallas_call(
        kernel,
        out_shape=outs,
        in_specs=[pl.BlockSpec(memory_space=pltpu.SMEM)] * len(scalars) + [IN_VMEM] * len(operands),
        out_specs=[IN_VMEM] * len(outs),
        compiler_params=pltpu.CompilerParams(vmem_limit_bytes=16 << 20),
        cost_estimate=pl.CostEstimate(
            flops=flops, bytes_accessed=moved, transcendentals=transcendentals
        ),
    )(*scalars, *operands)


def body(
    queries,
    key_vectors,
    head_value_vectors,
    head_sink_logits,
    out_weight,
    residual,
    norm_gain,
    router_weight,
    expert_ids,
    gate_weight,
    up_weight,
    down_weight,
    cotangent,
):
    tok_rows, chunk = residual.shape
    side, depth = lax.axis_size("y"), lax.axis_size("z")
    experts = router_weight.shape[1]
    capacity = 2 * TOPK * tok_rows // experts
    hidden_part = gate_weight.shape[2]

    place = lax.axis_index("f")
    core, chip = place & 1, place >> 1
    in_second_q = (chip == 1) | (chip == 2)
    units = -(-hidden_part // 16) * 16
    more_units = ((0, units - hidden_part), (0, 0))
    more_lanes = (more_units[0], (0, -D % 128))
    own_weights = jnp.concatenate(
        [jnp.pad(gate_weight[0].T, more_lanes), jnp.pad(up_weight[0].T, more_lanes)], axis=0
    )
    wide = -(-chunk // 128) * 128

    packed = jnp.concatenate([residual, expert_ids.astype(jnp.bfloat16)], axis=1)
    packed = swap_y_and_f(jnp.pad(packed, ((0, 0), (0, wide - chunk - TOPK))))
    gain_rest, gain_terms = norm_gain, []
    for _ in range(3):
        term = lax.reduce_precision(gain_rest, exponent_bits=8, mantissa_bits=7)
        gain_rest = gain_rest - term
        gain_terms.append(term.astype(jnp.bfloat16))
    features = jnp.concatenate([router_weight.T, jnp.stack(gain_terms)], axis=0)
    features = swap_y_and_f(jnp.pad(features, ((0, 13), (0, wide - chunk))))

    previous = from_previous_block(key_vectors, head_value_vectors)
    out_columns = double_stack(out_weight.T[None], "z")
    previous, out_columns = lax.optimization_barrier((previous, out_columns))
    attended = attend(queries, key_vectors, head_value_vectors, head_sink_logits, previous)
    attended, packed, own_weights = lax.optimization_barrier((attended, packed, own_weights))
    pair_weights = of_chip_pair(own_weights)
    attended_all = to_all(attended, "y").reshape(side * tok_rows, attended.shape[1])
    while out_columns.shape[0] < depth:
        out_columns = double_stack(out_columns, "z")
    out_columns = out_columns.reshape(chunk, out_weight.shape[0])
    out_columns = jnp.pad(out_columns, ((0, wide - chunk), (0, 0)))
    attended_all, features = lax.optimization_barrier((attended_all, features))

    partial_out = lax.dot_general(
        attended_all, out_columns, (((1,), (1,)), ((), ())), preferred_element_type=jnp.float32
    )
    partial_out = partial_out.astype(jnp.bfloat16).reshape(side, tok_rows, wide)
    parts = lax.all_to_all(partial_out, "f", split_axis=0, concat_axis=0, tiled=True)
    ids_here = packed[:tok_rows, chunk : chunk + TOPK].astype(jnp.int32)
    dest_here = places_of(ids_here, experts, capacity).T
    updated_here, local_slots = local_call(
        functools.partial(pack_kernel, chunk, experts),
        [
            jax.ShapeDtypeStruct((tok_rows, wide), jnp.float32),
            jax.ShapeDtypeStruct((experts * capacity, wide), jnp.bfloat16),
        ],
        (parts, packed, features, dest_here),
        flops=2 * experts * capacity * tok_rows * wide,
    )
    local_slots = local_slots.reshape(experts, capacity, wide)
    arrived = lax.all_to_all(local_slots, SEQ, split_axis=0, concat_axis=0, tiled=True)

    updated = swap_y_and_f(updated_here)[:, :chunk]
    dest = places_of(expert_ids, experts, capacity)
    slot_row = jnp.arange(experts * capacity, dtype=jnp.int32)
    placing = jnp.any(dest[:, :, None] == slot_row, axis=1).astype(jnp.bfloat16)

    expert_rows, sums = local_call(
        functools.partial(unpack_kernel, chunk),
        [
            jax.ShapeDtypeStruct((depth * capacity, -(-D // 128) * 128), jnp.bfloat16),
            jax.ShapeDtypeStruct((8, depth * capacity), jnp.float32),
        ],
        (arrived.reshape(side, depth * capacity, wide),),
        scalars=(lax.axis_index(SEQ).astype(jnp.int32)[None],),
    )
    own_gate = sums[:1].astype(jnp.bfloat16)
    other_rows = from_chip(expert_rows, Q_PARTNER)
    expert_rows, pair_weights = lax.optimization_barrier((expert_rows, pair_weights))
    core_weights = from_core(pair_weights)
    cotangent_slots = local_call(
        slots_kernel,
        [jax.ShapeDtypeStruct((experts * capacity, wide), jnp.bfloat16)],
        (dest.T, jnp.pad(cotangent, ((0, 0), (0, wide - chunk)))),
        flops=2 * experts * capacity * tok_rows * wide,
    )[0].reshape(experts, capacity, wide)
    other_rows, updated = lax.optimization_barrier((other_rows, updated))
    hidden_units = hidden_of(expert_rows, other_rows, [pair_weights, core_weights])
    hidden_units, cotangent_slots = lax.optimization_barrier((hidden_units, cotangent_slots))
    cotangent_arrived = lax.all_to_all(cotangent_slots, SEQ, split_axis=0, concat_axis=0, tiled=True)
    rows_per_device = depth * capacity
    hidden_units = ordered(hidden_units[0], hidden_units[1], core == 1, axis=1)
    hidden_units = hidden_units.reshape(4 * units, 2 * rows_per_device)
    hidden_units = jnp.where(
        in_second_q,
        jnp.concatenate(
            [hidden_units[:, rows_per_device:], hidden_units[:, :rows_per_device]], axis=1
        ),
        hidden_units,
    )
    gate_row = jnp.pad(own_gate, ((0, 15), (0, depth * capacity)))
    hidden_units = jnp.concatenate([hidden_units, gate_row], axis=0)
    gathered = lax.all_gather(hidden_units, "f", axis=0, tiled=True)

    device_at = {(P_OF[f // 2], Q_OF[f // 2], f % 2): f for f in range(8)}
    chips_with = [[x for x in range(4) if Q_OF[x] == q] for q in range(2)]
    down_rows = down_weight[0].reshape(side, hidden_part, chunk)
    down_rows = jnp.pad(down_rows, ((0, 0), *more_units)).reshape(side * units, chunk)
    expert_output = local_call(
        functools.partial(down_kernel, device_at, chips_with, 2 * units),
        [jax.ShapeDtypeStruct((side, depth * capacity, chunk), jnp.bfloat16)],
        (gathered, down_rows),
        flops=2 * experts * capacity * down_weight.shape[1] * chunk,
    )[0].reshape(experts, capacity, chunk)
    cotangent_arrived, expert_output = lax.optimization_barrier((cotangent_arrived, expert_output))
    returned = lax.all_to_all(expert_output, SEQ, split_axis=0, concat_axis=0, tiled=True)
    returned = returned.reshape(experts * capacity, chunk)
    mixture = jnp.dot(placing, returned, preferred_element_type=jnp.float32)
    layer_output = (updated + mixture).astype(jnp.bfloat16)
    grad_local = pl.pallas_call(
        functools.partial(grad_kernel, device_at, chips_with, 2 * units),
        out_shape=jax.ShapeDtypeStruct((side, hidden_part, chunk), jnp.bfloat16),
        in_specs=[IN_VMEM] * 2,
        out_specs=IN_VMEM,
        scratch_shapes=[pltpu.VMEM((experts * capacity, wide), jnp.bfloat16)],
        compiler_params=pltpu.CompilerParams(vmem_limit_bytes=16 << 20),
        cost_estimate=pl.CostEstimate(
            flops=2 * experts * capacity * side * units * wide,
            bytes_accessed=2 * (gathered.size + 2 * experts * capacity * wide),
            transcendentals=0,
        ),
    )(gathered, cotangent_arrived.reshape(experts * capacity, wide))
    return (layer_output, grad_local.reshape(1, side * hidden_part, chunk))


def solution(mesh):
    seq, ffn = mesh.devices.shape
    side = math.isqrt(seq)
    grid = Mesh(mesh.devices.reshape(side, seq // side, ffn), ("y", "z", "f"))
    return jax.shard_map(
        body,
        mesh=grid,
        in_specs=(
            P(SEQ, "f"),
            P(SEQ, "f"),
            P(SEQ, "f"),
            P("f"),
            P("f", SEQ),
            P(SEQ, "f"),
            P("f"),
            P("f", None),
            P(SEQ, None),
            P(SEQ, None, "f"),
            P(SEQ, None, "f"),
            P(SEQ, None, "f"),
            P(SEQ, "f"),
        ),
        out_specs=(P(SEQ, "f"), P(SEQ, None, "f")),
        check_vma=False,
    )
```

```python
import functools
import math

import jax
import jax.numpy as jnp
from jax import lax
from jax.experimental import pallas as pl
from jax.experimental.pallas import tpu as pltpu
from jax.sharding import Mesh, PartitionSpec as P

D = 2880
QUERY_HEADS = 64
KEY_VALUE_HEADS = 8
HEAD_SIZE = 64
VISIBLE_TOKENS = 128
TOPK = 4

SEQ = ("y", "z")
ROW_CONTRACT = (((0,), (0,)), ((), ()))


def from_previous_block(keys, values):
    count = lax.axis_size("y") * lax.axis_size("z")
    both = jnp.concatenate([keys, values], axis=1)
    both = lax.ppermute(both, SEQ, [(source, source + 1) for source in range(count - 1)])
    return both[:, : keys.shape[1]], both[:, keys.shape[1] :]


def swap_y_and_f(value):
    side, depth = lax.axis_size("y"), lax.axis_size("z")
    pairs = [
        ((y * depth + z) * side + f, (f * depth + z) * side + y)
        for y in range(side)
        for z in range(depth)
        for f in range(side)
    ]
    return lax.ppermute(value, ("y", "z", "f"), pairs)


def to_all(value, axis):
    copies = jnp.broadcast_to(value[None], (lax.axis_size(axis), *value.shape))
    return lax.all_to_all(copies, axis, split_axis=0, concat_axis=0, tiled=True)


def double_stack(stack, axis):
    step = stack.shape[0]
    count = lax.axis_size(axis)
    other = lax.ppermute(stack, axis, [(i, i ^ step) for i in range(count)])
    return ordered(stack, other, (lax.axis_index(axis) & step) != 0)


def ordered(mine, other, second, axis=0):
    return jnp.where(
        second,
        jnp.concatenate([other, mine], axis=axis),
        jnp.concatenate([mine, other], axis=axis),
    )


P_PARTNER = [3, 2, 1, 0]
Q_PARTNER = [1, 0, 3, 2]
P_OF = [0, 0, 1, 1]
Q_OF = [0, 1, 1, 0]


def from_core(value):
    return lax.ppermute(value, "f", [(f, f ^ 1) for f in range(8)])


def from_chip(value, partner):
    return lax.ppermute(value, "f", [(f, 2 * partner[f // 2] + f % 2) for f in range(8)])


def of_chip_pair(value):
    groups = [[f, 2 * P_PARTNER[f // 2] + f % 2] for f in range(8) if P_OF[f // 2] == 0]
    return lax.all_gather(value, "f", axis=0, axis_index_groups=groups, tiled=True)


def hidden_kernel(*refs):
    *row_refs, weight_ref, out_ref = refs
    aligned = D // 128 * 128
    rows = jnp.concatenate([ref[...] for ref in row_refs], axis=0)
    scale = jnp.sum(
        rows[:, aligned : aligned + 128].astype(jnp.float32).T[D - aligned : D - aligned + 3],
        axis=0,
        keepdims=True,
    )
    products = scale * lax.dot_general(
        weight_ref[...], rows, (((1,), (1,)), ((), ())), preferred_element_type=jnp.float32
    )
    units = weight_ref.shape[0] // 2
    gate_val, up_val = products[:units], products[units:]
    hidden = gate_val * jax.nn.sigmoid(1.702 * gate_val) * (up_val + 1.0)
    out_ref[0] = hidden.astype(jnp.bfloat16)


def hidden_of(row_blocks, weights):
    units = weights.shape[0] // 4
    count, width = row_blocks[0].shape
    total = count * len(row_blocks)
    whole = pl.BlockSpec((count, width), lambda p: (0, 0))
    return pl.pallas_call(
        hidden_kernel,
        grid=(2,),
        out_shape=jax.ShapeDtypeStruct((2, units, total), jnp.bfloat16),
        in_specs=[whole] * len(row_blocks) + [pl.BlockSpec((2 * units, width), lambda p: (p, 0))],
        out_specs=pl.BlockSpec((1, units, total), lambda p: (p, 0, 0)),
        compiler_params=pltpu.CompilerParams(vmem_limit_bytes=24 << 20),
        cost_estimate=pl.CostEstimate(
            flops=2 * total * weights.size,
            bytes_accessed=2 * (total * width + weights.size + 2 * units * total),
            transcendentals=2 * units * total,
        ),
    )(*row_blocks, weights)


def attend(queries, key_vectors, head_value_vectors, head_sink_logits, previous):
    tok_rows = queries.shape[0]
    key_heads = key_vectors.shape[1] // HEAD_SIZE
    query_grouping = QUERY_HEADS // KEY_VALUE_HEADS
    prev_keys, prev_values = previous
    all_keys = jnp.concatenate([prev_keys, key_vectors], axis=0).reshape(
        2 * tok_rows, key_heads, HEAD_SIZE
    )
    all_values = jnp.concatenate([prev_values, head_value_vectors], axis=0).reshape(
        2 * tok_rows, key_heads, HEAD_SIZE
    )
    query_heads = queries.reshape(tok_rows, key_heads, query_grouping, HEAD_SIZE)
    scores = jnp.einsum(
        "tkgd,skd->kgts", query_heads, all_keys, preferred_element_type=jnp.float32
    ) * HEAD_SIZE ** (-0.5)
    offset = lax.axis_index(SEQ) * tok_rows
    query_pos = offset + jnp.arange(tok_rows, dtype=jnp.int32)
    key_pos = offset - tok_rows + jnp.arange(2 * tok_rows, dtype=jnp.int32)
    valid = (
        (key_pos[None, :] >= 0)
        & (key_pos[None, :] <= query_pos[:, None])
        & (key_pos[None, :] > query_pos[:, None] - VISIBLE_TOKENS)
    )
    scores = jnp.where(valid, scores, -1e30)
    sink_entries = head_sink_logits.reshape(key_heads, query_grouping)[:, :, None]
    highest = jnp.maximum(jnp.max(scores, axis=-1), sink_entries)
    powers = jnp.exp(scores - highest[..., None])
    denom = jnp.sum(powers, axis=-1) + jnp.exp(sink_entries - highest)
    weights = (powers / denom[..., None]).astype(jnp.bfloat16)
    attended = jnp.einsum("kgts,skd->tkgd", weights, all_values, preferred_element_type=jnp.float32)
    return attended.astype(jnp.bfloat16).reshape(tok_rows, key_heads * query_grouping * HEAD_SIZE)


def places_of(ids, experts, capacity):
    tok_rows = ids.shape[0]
    onehot = (ids[:, :, None] == jnp.arange(experts, dtype=jnp.int32)).astype(jnp.float32)
    counts = jnp.sum(onehot, axis=1)
    row_index = jnp.arange(tok_rows, dtype=jnp.int32)
    strictly_lower = (row_index[:, None] > row_index[None, :]).astype(jnp.bfloat16)
    before = jnp.dot(
        strictly_lower, counts.astype(jnp.bfloat16), preferred_element_type=jnp.float32
    )
    slot = jnp.sum(onehot * before[:, None, :], axis=-1)
    return ids * capacity + slot.astype(jnp.int32)


def three_terms(value):
    terms = []
    for _ in range(3):
        term = value.astype(jnp.bfloat16).astype(jnp.float32)
        terms.append(term)
        value = value - term
    return terms


def to_slots(dest, rows, slots_ref):
    step = 256
    for start in range(0, slots_ref.shape[0], step):
        row = start + lax.broadcasted_iota(jnp.int32, (step, dest.shape[1]), 0)
        placing = (row == dest[0:1]).astype(jnp.float32)
        for j in range(1, TOPK):
            placing = placing + (row == dest[j : j + 1]).astype(jnp.float32)
        slots_ref[start : start + step, :] = jnp.dot(
            placing.astype(jnp.bfloat16), rows, preferred_element_type=jnp.float32
        ).astype(jnp.bfloat16)


def slots_kernel(dest_ref, rows_ref, slots_ref):
    to_slots(dest_ref[...], rows_ref[...], slots_ref)


def pack_kernel(
    spare, experts, parts_ref, packed_ref, features_ref, dest_ref, updated_ref, slots_ref
):
    aligned = spare // 128 * 128
    residual = packed_ref[...].astype(jnp.float32)
    column = lax.broadcasted_iota(jnp.int32, residual.shape, 1)
    updated = jnp.where(column < spare, residual, 0.0)
    for part in range(parts_ref.shape[0]):
        updated = updated + parts_ref[part].astype(jnp.float32)
    updated_ref[...] = updated
    gain = jnp.sum(features_ref[experts:].astype(jnp.float32), axis=0, keepdims=True)
    gained = updated * gain
    logits = lax.dot_general(
        gained,
        features_ref[:experts].astype(jnp.float32),
        (((1,), (1,)), ((), ())),
        precision=lax.Precision.HIGHEST,
        preferred_element_type=jnp.float32,
    )
    expert = lax.broadcasted_iota(jnp.int32, logits.shape, 1).astype(jnp.float32)
    last = gained[:, aligned:]
    lane = lax.broadcasted_iota(jnp.int32, last.shape, 1) - (spare - aligned)
    sums = [jnp.sum(updated * updated, axis=1, keepdims=True)]
    ids = []
    for j in range(TOPK):
        ids.append(
            jnp.sum(jnp.where(lane == j, residual[:, aligned:], 0.0), axis=1, keepdims=True)
        )
        sums.append(jnp.sum(jnp.where(expert == ids[j], logits, 0.0), axis=1, keepdims=True))
    terms = [three_terms(value) for value in sums]
    extras = [terms[i][k] for k in range(3) for i in range(1 + TOPK)]
    extras += [number + 1.0 for number in ids]
    for i, value in enumerate(extras):
        last = jnp.where(lane == i, value, last)
    rows = jnp.concatenate([gained[:, :aligned], last], axis=1).astype(jnp.bfloat16)
    to_slots(dest_ref[...], rows, slots_ref)


def unpack_kernel(spare, expert_ref, arrived_ref, rows_ref, side_ref):
    aligned = spare // 128 * 128
    first = arrived_ref[0][:, aligned:].astype(jnp.float32)
    total = first
    for chunk in range(arrived_ref.shape[0]):
        part = arrived_ref[chunk]
        if chunk:
            total = total + part[:, aligned:].astype(jnp.float32)
        rows_ref[:, chunk * spare : (chunk + 1) * spare] = part[:, :spare]
    lane = lax.broadcasted_iota(jnp.int32, total.shape, 1) - (spare - aligned)
    sums = []
    for i in range(1 + TOPK):
        wanted = (lane == i) | (lane == i + 1 + TOPK) | (lane == i + 2 * (1 + TOPK))
        sums.append(jnp.sum(jnp.where(wanted, total, 0.0), axis=1, keepdims=True))
    scale = lax.rsqrt(sums[0] / D + 1e-05)
    chosen = [value * scale for value in sums[1:]]
    highest = chosen[0]
    for value in chosen[1:]:
        highest = jnp.maximum(highest, value)
    powers = [jnp.exp(value - highest) for value in chosen]
    denom = sum(powers)
    own = (expert_ref[0] + 1).astype(jnp.float32)
    gate = jnp.zeros_like(scale)
    for j in range(TOPK):
        number = jnp.sum(
            jnp.where(lane == 3 * (1 + TOPK) + j, first, 0.0), axis=1, keepdims=True
        )
        gate = gate + jnp.where(number == own, powers[j] / denom, 0.0)
    column = lax.broadcasted_iota(jnp.int32, total.shape, 1)
    side_ref[...] = jnp.where(column == 0, gate, 0.0).T[: side_ref.shape[0]]
    column = column[:, : rows_ref.shape[1] - D]
    spare_columns = jnp.zeros(column.shape, jnp.float32)
    for i, term in enumerate(three_terms(scale)):
        spare_columns = jnp.where(column == i, term, spare_columns)
    rows_ref[:, D:] = spare_columns.astype(jnp.bfloat16)


def down_kernel(device_at, chips_with, units, hidden_ref, weight_ref, out_ref):
    height = hidden_ref.shape[0] // len(device_at)
    rows = out_ref.shape[1]
    for p in range(2):
        total = None
        for q in range(2):
            for c in range(2):
                start = device_at[p, q, c] * height
                for half, x in enumerate(chips_with[q]):
                    f = 2 * x + c
                    term = lax.dot_general(
                        hidden_ref[start + half * units : start + (half + 1) * units, :],
                        weight_ref[f * units : (f + 1) * units, :],
                        ROW_CONTRACT,
                        preferred_element_type=jnp.float32,
                    )
                    total = term if total is None else total + term
        for q in range(2):
            for c in range(2):
                f = device_at[p, q, c]
                gate = gate_column(hidden_ref, f * height + 2 * units, rows)
                block = total[(2 * q + c) * rows : (2 * q + c + 1) * rows]
                out_ref[f] = (block * gate).astype(jnp.bfloat16)


def gate_column(hidden_ref, start, rows):
    gate = hidden_ref[start : start + 16, :rows].astype(jnp.float32)[:1]
    return jnp.broadcast_to(gate, (rows, rows)).T[:, :1]


def grad_kernel(device_at, chips_with, units, hidden_ref, cotangent_ref, out_ref, grad_ref):
    height = hidden_ref.shape[0] // len(device_at)
    rows = cotangent_ref.shape[0] // len(device_at)
    kept, chunk = out_ref.shape[1:]
    order = [device_at[p, q, c] for p in range(2) for q in range(2) for c in range(2)]
    for i, f in enumerate(order):
        gate = gate_column(hidden_ref, f * height + 2 * units, rows)
        block = cotangent_ref[f * rows : (f + 1) * rows, :].astype(jnp.float32) * gate
        grad_ref[i * rows : (i + 1) * rows, :] = block.astype(jnp.bfloat16)
    for q in range(2):
        for half, x in enumerate(chips_with[q]):
            for c in range(2):
                total = None
                for p in range(2):
                    start = device_at[p, q, c] * height + half * units
                    term = jnp.dot(
                        hidden_ref[start : start + units, :],
                        grad_ref[4 * p * rows : 4 * (p + 1) * rows, :],
                        preferred_element_type=jnp.float32,
                    )
                    total = term if total is None else total + term
                out_ref[2 * x + c] = total[:kept, :chunk].astype(jnp.bfloat16)


IN_VMEM = pl.BlockSpec(memory_space=pltpu.VMEM)


def local_call(kernel, outs, operands, scalars=(), flops=0, transcendentals=0):
    moved = sum(x.size * x.dtype.itemsize for x in (*operands, *outs))
    return pl.pallas_call(
        kernel,
        out_shape=outs,
        in_specs=[pl.BlockSpec(memory_space=pltpu.SMEM)] * len(scalars) + [IN_VMEM] * len(operands),
        out_specs=[IN_VMEM] * len(outs),
        compiler_params=pltpu.CompilerParams(vmem_limit_bytes=16 << 20),
        cost_estimate=pl.CostEstimate(
            flops=flops, bytes_accessed=moved, transcendentals=transcendentals
        ),
    )(*scalars, *operands)


def body(
    queries,
    key_vectors,
    head_value_vectors,
    head_sink_logits,
    out_weight,
    residual,
    norm_gain,
    router_weight,
    expert_ids,
    gate_weight,
    up_weight,
    down_weight,
    cotangent,
):
    tok_rows, chunk = residual.shape
    side, depth = lax.axis_size("y"), lax.axis_size("z")
    experts = router_weight.shape[1]
    capacity = 2 * TOPK * tok_rows // experts
    hidden_part = gate_weight.shape[2]

    place = lax.axis_index("f")
    core, chip = place & 1, place >> 1
    in_second_q = (chip == 1) | (chip == 2)
    units = -(-hidden_part // 16) * 16
    more_units = ((0, units - hidden_part), (0, 0))
    more_lanes = (more_units[0], (0, -D % 128))
    own_weights = jnp.concatenate(
        [jnp.pad(gate_weight[0].T, more_lanes), jnp.pad(up_weight[0].T, more_lanes)], axis=0
    )
    wide = -(-chunk // 128) * 128

    packed = jnp.concatenate([residual, expert_ids.astype(jnp.bfloat16)], axis=1)
    packed = swap_y_and_f(jnp.pad(packed, ((0, 0), (0, wide - chunk - TOPK))))
    gain_rest, gain_terms = norm_gain, []
    for _ in range(3):
        term = lax.reduce_precision(gain_rest, exponent_bits=8, mantissa_bits=7)
        gain_rest = gain_rest - term
        gain_terms.append(term.astype(jnp.bfloat16))
    features = jnp.concatenate([router_weight.T, jnp.stack(gain_terms)], axis=0)
    features = swap_y_and_f(jnp.pad(features, ((0, 13), (0, wide - chunk))))

    key_vectors, own_weights = lax.optimization_barrier((key_vectors, own_weights))
    pair_weights = of_chip_pair(own_weights)
    previous = from_previous_block(key_vectors, head_value_vectors)
    out_columns = double_stack(out_weight.T[None], "z")
    previous, out_columns = lax.optimization_barrier((previous, out_columns))
    attended = attend(queries, key_vectors, head_value_vectors, head_sink_logits, previous)
    attended, packed = lax.optimization_barrier((attended, packed))
    attended_all = to_all(attended, "y").reshape(side * tok_rows, attended.shape[1])
    while out_columns.shape[0] < depth:
        out_columns = double_stack(out_columns, "z")
    out_columns = out_columns.reshape(chunk, out_weight.shape[0])
    out_columns = jnp.pad(out_columns, ((0, wide - chunk), (0, 0)))

    partial_out = lax.dot_general(
        attended_all, out_columns, (((1,), (1,)), ((), ())), preferred_element_type=jnp.float32
    )
    partial_out = partial_out.astype(jnp.bfloat16).reshape(side, tok_rows, wide)
    parts = lax.all_to_all(partial_out, "f", split_axis=0, concat_axis=0, tiled=True)
    ids_here = packed[:tok_rows, chunk : chunk + TOPK].astype(jnp.int32)
    dest_here = places_of(ids_here, experts, capacity).T
    updated_here, local_slots = local_call(
        functools.partial(pack_kernel, chunk, experts),
        [
            jax.ShapeDtypeStruct((tok_rows, wide), jnp.float32),
            jax.ShapeDtypeStruct((experts * capacity, wide), jnp.bfloat16),
        ],
        (parts, packed, features, dest_here),
        flops=2 * experts * capacity * tok_rows * wide,
    )
    local_slots = local_slots.reshape(experts, capacity, wide)
    arrived = lax.all_to_all(local_slots, SEQ, split_axis=0, concat_axis=0, tiled=True)

    updated = swap_y_and_f(updated_here)[:, :chunk]
    dest = places_of(expert_ids, experts, capacity)
    slot_row = jnp.arange(experts * capacity, dtype=jnp.int32)
    placing = jnp.any(dest[:, :, None] == slot_row, axis=1).astype(jnp.bfloat16)

    expert_rows, sums = local_call(
        functools.partial(unpack_kernel, chunk),
        [
            jax.ShapeDtypeStruct((depth * capacity, -(-D // 128) * 128), jnp.bfloat16),
            jax.ShapeDtypeStruct((8, depth * capacity), jnp.float32),
        ],
        (arrived.reshape(side, depth * capacity, wide),),
        scalars=(lax.axis_index(SEQ).astype(jnp.int32)[None],),
    )
    own_gate = sums[:1].astype(jnp.bfloat16)
    other_rows = from_chip(expert_rows, Q_PARTNER)
    core_rows = from_core(expert_rows)
    far_rows = from_core(other_rows)
    cotangent_slots = local_call(
        slots_kernel,
        [jax.ShapeDtypeStruct((experts * capacity, wide), jnp.bfloat16)],
        (dest.T, jnp.pad(cotangent, ((0, 0), (0, wide - chunk)))),
        flops=2 * experts * capacity * tok_rows * wide,
    )[0].reshape(experts, capacity, wide)
    hidden_units = hidden_of([expert_rows, core_rows, other_rows, far_rows], pair_weights)
    hidden_units, cotangent_slots = lax.optimization_barrier((hidden_units, cotangent_slots))
    cotangent_arrived = lax.all_to_all(cotangent_slots, SEQ, split_axis=0, concat_axis=0, tiled=True)
    rows_per_device = depth * capacity
    hidden_units = hidden_units.reshape(2 * units, 4 * rows_per_device)
    blocks = [
        hidden_units[:, i * rows_per_device : (i + 1) * rows_per_device] for i in range(4)
    ]
    hidden_units = ordered(
        ordered(blocks[0], blocks[1], core == 1, axis=1),
        ordered(blocks[2], blocks[3], core == 1, axis=1),
        in_second_q,
        axis=1,
    )
    gate_row = jnp.pad(own_gate, ((0, 15), (0, 3 * rows_per_device)))
    hidden_units = jnp.concatenate([hidden_units, gate_row], axis=0)
    gathered = lax.all_gather(hidden_units, "f", axis=0, tiled=True)
    gathered, updated = lax.optimization_barrier((gathered, updated))

    device_at = {(P_OF[f // 2], Q_OF[f // 2], f % 2): f for f in range(8)}
    chips_with = [[x for x in range(4) if Q_OF[x] == q] for q in range(2)]
    down_rows = down_weight[0].reshape(side, hidden_part, chunk)
    down_rows = jnp.pad(down_rows, ((0, 0), *more_units)).reshape(side * units, chunk)
    expert_output = local_call(
        functools.partial(down_kernel, device_at, chips_with, units),
        [jax.ShapeDtypeStruct((side, depth * capacity, chunk), jnp.bfloat16)],
        (gathered, down_rows),
        flops=2 * experts * capacity * down_weight.shape[1] * chunk,
    )[0].reshape(experts, capacity, chunk)
    cotangent_arrived, expert_output = lax.optimization_barrier((cotangent_arrived, expert_output))
    returned = lax.all_to_all(expert_output, SEQ, split_axis=0, concat_axis=0, tiled=True)
    returned = returned.reshape(experts * capacity, chunk)
    mixture = jnp.dot(placing, returned, preferred_element_type=jnp.float32)
    layer_output = (updated + mixture).astype(jnp.bfloat16)
    grad_local = pl.pallas_call(
        functools.partial(grad_kernel, device_at, chips_with, units),
        out_shape=jax.ShapeDtypeStruct((side, hidden_part, chunk), jnp.bfloat16),
        in_specs=[IN_VMEM] * 2,
        out_specs=IN_VMEM,
        scratch_shapes=[pltpu.VMEM((experts * capacity, wide), jnp.bfloat16)],
        compiler_params=pltpu.CompilerParams(vmem_limit_bytes=16 << 20),
        cost_estimate=pl.CostEstimate(
            flops=2 * experts * capacity * side * units * wide,
            bytes_accessed=2 * (gathered.size + 2 * experts * capacity * wide),
            transcendentals=0,
        ),
    )(gathered, cotangent_arrived.reshape(experts * capacity, wide))
    return (layer_output, grad_local.reshape(1, side * hidden_part, chunk))


def solution(mesh):
    seq, ffn = mesh.devices.shape
    side = math.isqrt(seq)
    grid = Mesh(mesh.devices.reshape(side, seq // side, ffn), ("y", "z", "f"))
    return jax.shard_map(
        body,
        mesh=grid,
        in_specs=(
            P(SEQ, "f"),
            P(SEQ, "f"),
            P(SEQ, "f"),
            P("f"),
            P("f", SEQ),
            P(SEQ, "f"),
            P("f"),
            P("f", None),
            P(SEQ, None),
            P(SEQ, None, "f"),
            P(SEQ, None, "f"),
            P(SEQ, None, "f"),
            P(SEQ, "f"),
        ),
        out_specs=(P(SEQ, "f"), P(SEQ, None, "f")),
        check_vma=False,
    )
```

```python
import functools
import math

import jax
import jax.numpy as jnp
from jax import lax
from jax.experimental import pallas as pl
from jax.experimental.pallas import tpu as pltpu
from jax.sharding import Mesh, PartitionSpec as P

D = 2880
QUERY_HEADS = 64
KEY_VALUE_HEADS = 8
HEAD_SIZE = 64
VISIBLE_TOKENS = 128
TOPK = 4

SEQ = ("y", "z")
ROW_CONTRACT = (((0,), (0,)), ((), ()))


def from_previous_block(keys, values):
    count = lax.axis_size("y") * lax.axis_size("z")
    both = jnp.concatenate([keys, values], axis=1)
    both = lax.ppermute(both, SEQ, [(source, source + 1) for source in range(count - 1)])
    return both[:, : keys.shape[1]], both[:, keys.shape[1] :]


def swap_y_and_f(value):
    side, depth = lax.axis_size("y"), lax.axis_size("z")
    pairs = [
        ((y * depth + z) * side + f, (f * depth + z) * side + y)
        for y in range(side)
        for z in range(depth)
        for f in range(side)
    ]
    return lax.ppermute(value, ("y", "z", "f"), pairs)


def to_all(value, axis):
    copies = jnp.broadcast_to(value[None], (lax.axis_size(axis), *value.shape))
    return lax.all_to_all(copies, axis, split_axis=0, concat_axis=0, tiled=True)


def double_stack(stack, axis):
    step = stack.shape[0]
    count = lax.axis_size(axis)
    other = lax.ppermute(stack, axis, [(i, i ^ step) for i in range(count)])
    return ordered(stack, other, (lax.axis_index(axis) & step) != 0)


def ordered(mine, other, second, axis=0):
    return jnp.where(
        second,
        jnp.concatenate([other, mine], axis=axis),
        jnp.concatenate([mine, other], axis=axis),
    )


P_PARTNER = [3, 2, 1, 0]
Q_PARTNER = [1, 0, 3, 2]
P_OF = [0, 0, 1, 1]
Q_OF = [0, 1, 1, 0]


def from_core(value):
    return lax.ppermute(value, "f", [(f, f ^ 1) for f in range(8)])


def from_chip(value, partner):
    return lax.ppermute(value, "f", [(f, 2 * partner[f // 2] + f % 2) for f in range(8)])


def of_chip_pair(value):
    groups = [[f, 2 * P_PARTNER[f // 2] + f % 2] for f in range(8) if P_OF[f // 2] == 0]
    return lax.all_gather(value, "f", axis=0, axis_index_groups=groups, tiled=True)


def hidden_kernel(*refs):
    *row_refs, weight_ref, out_ref = refs
    aligned = D // 128 * 128
    rows = jnp.concatenate([ref[...] for ref in row_refs], axis=0)
    scale = jnp.sum(
        rows[:, aligned : aligned + 128].astype(jnp.float32).T[D - aligned : D - aligned + 3],
        axis=0,
        keepdims=True,
    )
    products = scale * lax.dot_general(
        weight_ref[...], rows, (((1,), (1,)), ((), ())), preferred_element_type=jnp.float32
    )
    units = weight_ref.shape[0] // 2
    gate_val, up_val = products[:units], products[units:]
    hidden = gate_val * jax.nn.sigmoid(1.702 * gate_val) * (up_val + 1.0)
    out_ref[0] = hidden.astype(jnp.bfloat16)


def hidden_of(row_blocks, weights):
    units = weights.shape[0] // 4
    count, width = row_blocks[0].shape
    total = count * len(row_blocks)
    whole = pl.BlockSpec((count, width), lambda p: (0, 0))
    return pl.pallas_call(
        hidden_kernel,
        grid=(2,),
        out_shape=jax.ShapeDtypeStruct((2, units, total), jnp.bfloat16),
        in_specs=[whole] * len(row_blocks) + [pl.BlockSpec((2 * units, width), lambda p: (p, 0))],
        out_specs=pl.BlockSpec((1, units, total), lambda p: (p, 0, 0)),
        compiler_params=pltpu.CompilerParams(vmem_limit_bytes=24 << 20),
        cost_estimate=pl.CostEstimate(
            flops=2 * total * weights.size,
            bytes_accessed=2 * (total * width + weights.size + 2 * units * total),
            transcendentals=2 * units * total,
        ),
    )(*row_blocks, weights)


def attend(queries, key_vectors, head_value_vectors, head_sink_logits, previous):
    tok_rows = queries.shape[0]
    key_heads = key_vectors.shape[1] // HEAD_SIZE
    query_grouping = QUERY_HEADS // KEY_VALUE_HEADS
    prev_keys, prev_values = previous
    all_keys = jnp.concatenate([prev_keys, key_vectors], axis=0).reshape(
        2 * tok_rows, key_heads, HEAD_SIZE
    )
    all_values = jnp.concatenate([prev_values, head_value_vectors], axis=0).reshape(
        2 * tok_rows, key_heads, HEAD_SIZE
    )
    query_heads = queries.reshape(tok_rows, key_heads, query_grouping, HEAD_SIZE)
    scores = jnp.einsum(
        "tkgd,skd->kgts", query_heads, all_keys, preferred_element_type=jnp.float32
    ) * HEAD_SIZE ** (-0.5)
    offset = lax.axis_index(SEQ) * tok_rows
    query_pos = offset + jnp.arange(tok_rows, dtype=jnp.int32)
    key_pos = offset - tok_rows + jnp.arange(2 * tok_rows, dtype=jnp.int32)
    valid = (
        (key_pos[None, :] >= 0)
        & (key_pos[None, :] <= query_pos[:, None])
        & (key_pos[None, :] > query_pos[:, None] - VISIBLE_TOKENS)
    )
    scores = jnp.where(valid, scores, -1e30)
    sink_entries = head_sink_logits.reshape(key_heads, query_grouping)[:, :, None]
    highest = jnp.maximum(jnp.max(scores, axis=-1), sink_entries)
    powers = jnp.exp(scores - highest[..., None])
    denom = jnp.sum(powers, axis=-1) + jnp.exp(sink_entries - highest)
    weights = (powers / denom[..., None]).astype(jnp.bfloat16)
    attended = jnp.einsum("kgts,skd->tkgd", weights, all_values, preferred_element_type=jnp.float32)
    return attended.astype(jnp.bfloat16).reshape(tok_rows, key_heads * query_grouping * HEAD_SIZE)


def places_of(ids, experts, capacity):
    tok_rows = ids.shape[0]
    onehot = (ids[:, :, None] == jnp.arange(experts, dtype=jnp.int32)).astype(jnp.float32)
    counts = jnp.sum(onehot, axis=1)
    row_index = jnp.arange(tok_rows, dtype=jnp.int32)
    strictly_lower = (row_index[:, None] > row_index[None, :]).astype(jnp.bfloat16)
    before = jnp.dot(
        strictly_lower, counts.astype(jnp.bfloat16), preferred_element_type=jnp.float32
    )
    slot = jnp.sum(onehot * before[:, None, :], axis=-1)
    return ids * capacity + slot.astype(jnp.int32)


def three_terms(value):
    terms = []
    for _ in range(3):
        term = value.astype(jnp.bfloat16).astype(jnp.float32)
        terms.append(term)
        value = value - term
    return terms


def to_slots(dest, rows, slots_ref):
    step = 256
    for start in range(0, slots_ref.shape[0], step):
        row = start + lax.broadcasted_iota(jnp.int32, (step, dest.shape[1]), 0)
        placing = (row == dest[0:1]).astype(jnp.float32)
        for j in range(1, TOPK):
            placing = placing + (row == dest[j : j + 1]).astype(jnp.float32)
        slots_ref[start : start + step, :] = jnp.dot(
            placing.astype(jnp.bfloat16), rows, preferred_element_type=jnp.float32
        ).astype(jnp.bfloat16)


def slots_kernel(dest_ref, rows_ref, slots_ref):
    to_slots(dest_ref[...], rows_ref[...], slots_ref)


def pack_kernel(
    spare, experts, parts_ref, packed_ref, features_ref, dest_ref, updated_ref, slots_ref
):
    aligned = spare // 128 * 128
    residual = packed_ref[...].astype(jnp.float32)
    column = lax.broadcasted_iota(jnp.int32, residual.shape, 1)
    updated = jnp.where(column < spare, residual, 0.0)
    for part in range(parts_ref.shape[0]):
        updated = updated + parts_ref[part].astype(jnp.float32)
    updated_ref[...] = updated
    gain = jnp.sum(features_ref[experts:].astype(jnp.float32), axis=0, keepdims=True)
    gained = updated * gain
    logits = lax.dot_general(
        gained,
        features_ref[:experts].astype(jnp.float32),
        (((1,), (1,)), ((), ())),
        precision=lax.Precision.HIGHEST,
        preferred_element_type=jnp.float32,
    )
    expert = lax.broadcasted_iota(jnp.int32, logits.shape, 1).astype(jnp.float32)
    last = gained[:, aligned:]
    lane = lax.broadcasted_iota(jnp.int32, last.shape, 1) - (spare - aligned)
    sums = [jnp.sum(updated * updated, axis=1, keepdims=True)]
    ids = []
    for j in range(TOPK):
        ids.append(
            jnp.sum(jnp.where(lane == j, residual[:, aligned:], 0.0), axis=1, keepdims=True)
        )
        sums.append(jnp.sum(jnp.where(expert == ids[j], logits, 0.0), axis=1, keepdims=True))
    terms = [three_terms(value) for value in sums]
    extras = [terms[i][k] for k in range(3) for i in range(1 + TOPK)]
    extras += [number + 1.0 for number in ids]
    for i, value in enumerate(extras):
        last = jnp.where(lane == i, value, last)
    rows = jnp.concatenate([gained[:, :aligned], last], axis=1).astype(jnp.bfloat16)
    to_slots(dest_ref[...], rows, slots_ref)


def unpack_kernel(spare, expert_ref, arrived_ref, rows_ref, side_ref):
    aligned = spare // 128 * 128
    first = arrived_ref[0][:, aligned:].astype(jnp.float32)
    total = first
    for chunk in range(arrived_ref.shape[0]):
        part = arrived_ref[chunk]
        if chunk:
            total = total + part[:, aligned:].astype(jnp.float32)
        rows_ref[:, chunk * spare : (chunk + 1) * spare] = part[:, :spare]
    lane = lax.broadcasted_iota(jnp.int32, total.shape, 1) - (spare - aligned)
    sums = []
    for i in range(1 + TOPK):
        wanted = (lane == i) | (lane == i + 1 + TOPK) | (lane == i + 2 * (1 + TOPK))
        sums.append(jnp.sum(jnp.where(wanted, total, 0.0), axis=1, keepdims=True))
    scale = lax.rsqrt(sums[0] / D + 1e-05)
    chosen = [value * scale for value in sums[1:]]
    highest = chosen[0]
    for value in chosen[1:]:
        highest = jnp.maximum(highest, value)
    powers = [jnp.exp(value - highest) for value in chosen]
    denom = sum(powers)
    own = (expert_ref[0] + 1).astype(jnp.float32)
    gate = jnp.zeros_like(scale)
    for j in range(TOPK):
        number = jnp.sum(
            jnp.where(lane == 3 * (1 + TOPK) + j, first, 0.0), axis=1, keepdims=True
        )
        gate = gate + jnp.where(number == own, powers[j] / denom, 0.0)
    column = lax.broadcasted_iota(jnp.int32, total.shape, 1)
    side_ref[...] = jnp.where(column == 0, gate, 0.0).T[: side_ref.shape[0]]
    column = column[:, : rows_ref.shape[1] - D]
    spare_columns = jnp.zeros(column.shape, jnp.float32)
    for i, term in enumerate(three_terms(scale)):
        spare_columns = jnp.where(column == i, term, spare_columns)
    rows_ref[:, D:] = spare_columns.astype(jnp.bfloat16)


def down_kernel(device_at, chips_with, units, hidden_ref, weight_ref, out_ref):
    height = hidden_ref.shape[0] // len(device_at)
    rows = out_ref.shape[1]
    for p in range(2):
        total = None
        for q in range(2):
            for c in range(2):
                start = device_at[p, q, c] * height
                for half, x in enumerate(chips_with[q]):
                    f = 2 * x + c
                    term = lax.dot_general(
                        hidden_ref[start + half * units : start + (half + 1) * units, :],
                        weight_ref[f * units : (f + 1) * units, :],
                        ROW_CONTRACT,
                        preferred_element_type=jnp.float32,
                    )
                    total = term if total is None else total + term
        for q in range(2):
            for c in range(2):
                f = device_at[p, q, c]
                gate = gate_column(hidden_ref, f * height + 2 * units, rows)
                block = total[(2 * q + c) * rows : (2 * q + c + 1) * rows]
                out_ref[f] = (block * gate).astype(jnp.bfloat16)


def gate_column(hidden_ref, start, rows):
    gate = hidden_ref[start : start + 16, :rows].astype(jnp.float32)[:1]
    return jnp.broadcast_to(gate, (rows, rows)).T[:, :1]


def grad_kernel(device_at, chips_with, units, hidden_ref, cotangent_ref, out_ref, grad_ref):
    height = hidden_ref.shape[0] // len(device_at)
    rows = cotangent_ref.shape[0] // len(device_at)
    kept, chunk = out_ref.shape[1:]
    order = [device_at[p, q, c] for p in range(2) for q in range(2) for c in range(2)]
    for i, f in enumerate(order):
        gate = gate_column(hidden_ref, f * height + 2 * units, rows)
        block = cotangent_ref[f * rows : (f + 1) * rows, :].astype(jnp.float32) * gate
        grad_ref[i * rows : (i + 1) * rows, :] = block.astype(jnp.bfloat16)
    for q in range(2):
        for half, x in enumerate(chips_with[q]):
            for c in range(2):
                total = None
                for p in range(2):
                    start = device_at[p, q, c] * height + half * units
                    term = jnp.dot(
                        hidden_ref[start : start + units, :],
                        grad_ref[4 * p * rows : 4 * (p + 1) * rows, :],
                        preferred_element_type=jnp.float32,
                    )
                    total = term if total is None else total + term
                out_ref[2 * x + c] = total[:kept, :chunk].astype(jnp.bfloat16)


IN_VMEM = pl.BlockSpec(memory_space=pltpu.VMEM)


def local_call(kernel, outs, operands, scalars=(), flops=0, transcendentals=0):
    moved = sum(x.size * x.dtype.itemsize for x in (*operands, *outs))
    return pl.pallas_call(
        kernel,
        out_shape=outs,
        in_specs=[pl.BlockSpec(memory_space=pltpu.SMEM)] * len(scalars) + [IN_VMEM] * len(operands),
        out_specs=[IN_VMEM] * len(outs),
        compiler_params=pltpu.CompilerParams(vmem_limit_bytes=16 << 20),
        cost_estimate=pl.CostEstimate(
            flops=flops, bytes_accessed=moved, transcendentals=transcendentals
        ),
    )(*scalars, *operands)


def body(
    queries,
    key_vectors,
    head_value_vectors,
    head_sink_logits,
    out_weight,
    residual,
    norm_gain,
    router_weight,
    expert_ids,
    gate_weight,
    up_weight,
    down_weight,
    cotangent,
):
    tok_rows, chunk = residual.shape
    side, depth = lax.axis_size("y"), lax.axis_size("z")
    experts = router_weight.shape[1]
    capacity = 2 * TOPK * tok_rows // experts
    hidden_part = gate_weight.shape[2]

    place = lax.axis_index("f")
    core, chip = place & 1, place >> 1
    in_second_q = (chip == 1) | (chip == 2)
    units = -(-hidden_part // 16) * 16
    more_units = ((0, units - hidden_part), (0, 0))
    more_lanes = (more_units[0], (0, -D % 128))
    own_weights = jnp.concatenate(
        [jnp.pad(gate_weight[0].T, more_lanes), jnp.pad(up_weight[0].T, more_lanes)], axis=0
    )
    wide = -(-chunk // 128) * 128

    packed = jnp.concatenate([residual, expert_ids.astype(jnp.bfloat16)], axis=1)
    packed = swap_y_and_f(jnp.pad(packed, ((0, 0), (0, wide - chunk - TOPK))))
    gain_rest, gain_terms = norm_gain, []
    for _ in range(3):
        term = lax.reduce_precision(gain_rest, exponent_bits=8, mantissa_bits=7)
        gain_rest = gain_rest - term
        gain_terms.append(term.astype(jnp.bfloat16))
    features = jnp.concatenate([router_weight.T, jnp.stack(gain_terms)], axis=0)
    features = swap_y_and_f(jnp.pad(features, ((0, 13), (0, wide - chunk))))

    key_vectors, own_weights = lax.optimization_barrier((key_vectors, own_weights))
    pair_weights = of_chip_pair(own_weights)
    previous = from_previous_block(key_vectors, head_value_vectors)
    out_columns = double_stack(out_weight.T[None], "z")
    previous, out_columns = lax.optimization_barrier((previous, out_columns))
    attended = attend(queries, key_vectors, head_value_vectors, head_sink_logits, previous)
    attended, packed = lax.optimization_barrier((attended, packed))
    attended_all = to_all(attended, "y").reshape(side * tok_rows, attended.shape[1])
    while out_columns.shape[0] < depth:
        out_columns = double_stack(out_columns, "z")
    out_columns = out_columns.reshape(chunk, out_weight.shape[0])
    out_columns = jnp.pad(out_columns, ((0, wide - chunk), (0, 0)))

    partial_out = lax.dot_general(
        attended_all, out_columns, (((1,), (1,)), ((), ())), preferred_element_type=jnp.float32
    )
    partial_out = partial_out.astype(jnp.bfloat16).reshape(side, tok_rows, wide)
    parts = lax.all_to_all(partial_out, "f", split_axis=0, concat_axis=0, tiled=True)
    ids_here = packed[:tok_rows, chunk : chunk + TOPK].astype(jnp.int32)
    dest_here = places_of(ids_here, experts, capacity).T
    updated_here, local_slots = local_call(
        functools.partial(pack_kernel, chunk, experts),
        [
            jax.ShapeDtypeStruct((tok_rows, wide), jnp.float32),
            jax.ShapeDtypeStruct((experts * capacity, wide), jnp.bfloat16),
        ],
        (parts, packed, features, dest_here),
        flops=2 * experts * capacity * tok_rows * wide,
    )
    local_slots = local_slots.reshape(experts, capacity, wide)
    arrived = lax.all_to_all(local_slots, SEQ, split_axis=0, concat_axis=0, tiled=True)

    updated = swap_y_and_f(updated_here.astype(jnp.bfloat16))[:, :chunk].astype(jnp.float32)
    dest = places_of(expert_ids, experts, capacity)
    slot_row = jnp.arange(experts * capacity, dtype=jnp.int32)
    placing = jnp.any(dest[:, :, None] == slot_row, axis=1).astype(jnp.bfloat16)

    expert_rows, sums = local_call(
        functools.partial(unpack_kernel, chunk),
        [
            jax.ShapeDtypeStruct((depth * capacity, -(-D // 128) * 128), jnp.bfloat16),
            jax.ShapeDtypeStruct((8, depth * capacity), jnp.float32),
        ],
        (arrived.reshape(side, depth * capacity, wide),),
        scalars=(lax.axis_index(SEQ).astype(jnp.int32)[None],),
    )
    own_gate = sums[:1].astype(jnp.bfloat16)
    other_rows = from_chip(expert_rows, Q_PARTNER)
    core_rows = from_core(expert_rows)
    far_rows = from_core(other_rows)
    cotangent_slots = local_call(
        slots_kernel,
        [jax.ShapeDtypeStruct((experts * capacity, wide), jnp.bfloat16)],
        (dest.T, jnp.pad(cotangent, ((0, 0), (0, wide - chunk)))),
        flops=2 * experts * capacity * tok_rows * wide,
    )[0].reshape(experts, capacity, wide)
    hidden_units = hidden_of([expert_rows, core_rows, other_rows, far_rows], pair_weights)
    hidden_units, cotangent_slots = lax.optimization_barrier((hidden_units, cotangent_slots))
    cotangent_arrived = lax.all_to_all(cotangent_slots, SEQ, split_axis=0, concat_axis=0, tiled=True)
    rows_per_device = depth * capacity
    hidden_units = hidden_units.reshape(2 * units, 4 * rows_per_device)
    blocks = [
        hidden_units[:, i * rows_per_device : (i + 1) * rows_per_device] for i in range(4)
    ]
    hidden_units = ordered(
        ordered(blocks[0], blocks[1], core == 1, axis=1),
        ordered(blocks[2], blocks[3], core == 1, axis=1),
        in_second_q,
        axis=1,
    )
    gate_row = jnp.pad(own_gate, ((0, 15), (0, 3 * rows_per_device)))
    hidden_units = jnp.concatenate([hidden_units, gate_row], axis=0)
    gathered = lax.all_gather(hidden_units, "f", axis=0, tiled=True)
    gathered, updated = lax.optimization_barrier((gathered, updated))

    device_at = {(P_OF[f // 2], Q_OF[f // 2], f % 2): f for f in range(8)}
    chips_with = [[x for x in range(4) if Q_OF[x] == q] for q in range(2)]
    down_rows = down_weight[0].reshape(side, hidden_part, chunk)
    down_rows = jnp.pad(down_rows, ((0, 0), *more_units)).reshape(side * units, chunk)
    expert_output = local_call(
        functools.partial(down_kernel, device_at, chips_with, units),
        [jax.ShapeDtypeStruct((side, depth * capacity, chunk), jnp.bfloat16)],
        (gathered, down_rows),
        flops=2 * experts * capacity * down_weight.shape[1] * chunk,
    )[0].reshape(experts, capacity, chunk)
    cotangent_arrived, expert_output = lax.optimization_barrier((cotangent_arrived, expert_output))
    returned = lax.all_to_all(expert_output, SEQ, split_axis=0, concat_axis=0, tiled=True)
    returned = returned.reshape(experts * capacity, chunk)
    mixture = jnp.dot(placing, returned, preferred_element_type=jnp.float32)
    layer_output = (updated + mixture).astype(jnp.bfloat16)
    grad_local = pl.pallas_call(
        functools.partial(grad_kernel, device_at, chips_with, units),
        out_shape=jax.ShapeDtypeStruct((side, hidden_part, chunk), jnp.bfloat16),
        in_specs=[IN_VMEM] * 2,
        out_specs=IN_VMEM,
        scratch_shapes=[pltpu.VMEM((experts * capacity, wide), jnp.bfloat16)],
        compiler_params=pltpu.CompilerParams(vmem_limit_bytes=16 << 20),
        cost_estimate=pl.CostEstimate(
            flops=2 * experts * capacity * side * units * wide,
            bytes_accessed=2 * (gathered.size + 2 * experts * capacity * wide),
            transcendentals=0,
        ),
    )(gathered, cotangent_arrived.reshape(experts * capacity, wide))
    return (layer_output, grad_local.reshape(1, side * hidden_part, chunk))


def solution(mesh):
    seq, ffn = mesh.devices.shape
    side = math.isqrt(seq)
    grid = Mesh(mesh.devices.reshape(side, seq // side, ffn), ("y", "z", "f"))
    return jax.shard_map(
        body,
        mesh=grid,
        in_specs=(
            P(SEQ, "f"),
            P(SEQ, "f"),
            P(SEQ, "f"),
            P("f"),
            P("f", SEQ),
            P(SEQ, "f"),
            P("f"),
            P("f", None),
            P(SEQ, None),
            P(SEQ, None, "f"),
            P(SEQ, None, "f"),
            P(SEQ, None, "f"),
            P(SEQ, "f"),
        ),
        out_specs=(P(SEQ, "f"), P(SEQ, None, "f")),
        check_vma=False,
    )
```
